32 devices in a mesh: parts: 2 (over y), tile: 4 (over z), slab: 4 (over x, core).
Axes of the slice: x: 2, y: 2, z: 4, core: 2. Of those that a mesh axis runs over, the one named last changes fastest.
Arguments:
- amps: bfloat16 [4, 32, 64, 64, 512], P('slab', 'tile', None, 'parts'), parts along dimension 3, may hold values from -6 to 6
- integrals: bfloat16 [4, 2048, 2, 2048], P('slab', None, 'parts'), parts along dimension 2, may hold values from -0.09375 to 0.09375
- tile_mask: int32 [4, 64, 32], P('slab', 'parts'), parts along dimension 1, may hold values from 0 to 1, as said below
- amp_map: int32 [32], replicated, may hold values from 0 to 31, each once
- con_map: int32 [32], replicated, may hold values from 0 to 31, each once
Outputs:
- residual: bfloat16 [2048, 2, 32, 512], P('slab', 'parts', 'tile'), parts along dimension 1
The draws below stay inside these ranges and needn't reach their ends.
There are 2 independent parts, one for each index of `parts`. The reference program is written for one: setup_inputs(seed, part) draws one part's arguments, and reference() takes and returns one part's arrays. A program takes and returns all parts, laid end to end along the dimension named above; an argument that names none is the same for every part. Nothing has to cross between parts.
Inputs may be any that keep to these rules, and one draw needn't show every extreme that they name: `tile_mask`: each row (a k tile and an a tile) has between half of 24 and 24 ones, and each k tile has a row with exactly 24. `amp_map`: a permutation of the virtual tiles. `con_map`: a permutation of the virtual tiles.
All inputs are finite; a program needn't handle non-finite values.
Results may differ from the reference program's by a relative error of at most 0.001.
Values may be sent and summed in bfloat16 or wider, within the bound.
A program may use at most 192 MiB of HBM per device.

```python
import jax
import jax.numpy as jnp
from jax import lax

V = 2048
TS = 64
NVT = 32
MAXNZ = 24
OI = 8
OJ = 1
KW = 1
KO = 4
N_SLAB = 4


def draw_tile_mask(key, part):
    key = jax.random.fold_in(key, 11)
    first_key, second_key, third_key = jax.random.split(key, 3)
    counts = jax.random.randint(first_key, (N_SLAB, NVT), MAXNZ // 2, MAXNZ + 1)
    fullest = jax.random.randint(second_key, (N_SLAB, 1), 0, NVT)
    counts = jnp.where(jnp.arange(NVT)[None, :] == fullest, MAXNZ, counts)
    row_keys = jax.random.split(third_key, N_SLAB * NVT)
    ranking = jax.vmap(lambda row_key: jax.random.permutation(row_key, NVT))(row_keys)
    ranking = ranking.reshape(N_SLAB, NVT, NVT)
    return (ranking < counts[:, :, None]).astype(jnp.int32)


def shard_levels(rng, shape, cuts, low, top_value):
    def one(dim, parts):
        draws = jax.random.uniform(jax.random.fold_in(jax.random.fold_in(rng, 6), dim), (parts,), jnp.float32, low / len(cuts), top_value / len(cuts))
        return jnp.repeat(jnp.exp(draws), shape[dim] // parts).reshape((-1,) + (1,) * (len(shape) - dim - 1))

    level = one(*cuts[0])
    for cut in cuts[1:]:
        level = level * one(*cut)
    return level


def centred(stream_key, extent, width, most, cuts=(), kind=jnp.bfloat16):
    drawn = jax.random.normal(stream_key, extent, jnp.float32) * width
    if len(cuts) > 0:
        drawn = shard_levels(stream_key, extent, cuts, -0.22, 0.18) * drawn
    return jnp.clip(drawn, min=-most, max=most).astype(kind)


def setup_inputs(seed: int = 0, part: int = 0) -> dict:
    keys = jax.random.split(jax.random.key(seed), 6)
    part_keys = jax.random.split(jax.random.fold_in(keys[5], part), 6)
    return {
        "amps": centred(part_keys[0], (KO, NVT, TS, NVT, OI * TS), 1.0, 6.0, ((0, 4), (1, 4))),
        "integrals": centred(part_keys[1], (KO, V, OJ, V), (KO * V // 2) ** -0.5, 0.09375, ((0, 4),)),
        "tile_mask": draw_tile_mask(jax.random.fold_in(jax.random.fold_in(keys[5], part), 71), part),
        "amp_map": jax.random.permutation(keys[3], NVT).astype(jnp.int32),
        "con_map": jax.random.permutation(keys[4], NVT).astype(jnp.int32),
    }


def reference(amps, integrals, tile_mask, amp_map, con_map):
    inverse = jnp.argsort(amp_map).astype(jnp.int32)
    natural = jnp.take(amps, inverse, axis=1)
    k_total = amps.shape[0]

    def accumulate(summed, level):
        block = lax.dynamic_index_in_dim(natural, level, 0, keepdims=False)
        mask_now = lax.dynamic_index_in_dim(tile_mask, level // KW, 0, keepdims=False)
        scaled = block * jnp.transpose(mask_now)[:, None, :, None].astype(block.dtype)
        factor_t = scaled.reshape(V, NVT * OI * TS)
        factor_w = lax.dynamic_index_in_dim(integrals, level, 0, keepdims=False).reshape(V * OJ, V)
        return summed + jnp.dot(factor_w, factor_t, preferred_element_type=jnp.float32), None

    start_value = jnp.zeros((V * OJ, NVT * OI * TS), jnp.float32)
    summed, unused = lax.scan(accumulate, start_value, jnp.arange(k_total, dtype=jnp.int32))
    result = jnp.take(summed.reshape(V, OJ, NVT, OI * TS), con_map, axis=2)
    return result.astype(jnp.bfloat16)
```

```python
import functools

import jax
import jax.numpy as jnp
from jax import lax
from jax.experimental import pallas as pl
from jax.experimental.pallas import tpu as pltpu
from jax.sharding import PartitionSpec as P

MESH = pl.DeviceIdType.MESH
GROUP = 16
CHUNK = 256
AHEAD = 2


def arrange(nvt, ts, width, target_ref, amps_ref, out_ref):
    rows = GROUP * nvt
    column = lax.broadcasted_iota(jnp.int32, (rows, rows), 1)
    select = jnp.where(column == target_ref[0], 1.0, 0.0).astype(jnp.bfloat16)
    for part in range(ts // GROUP):
        block = amps_ref[pl.ds(part * rows, rows), :]
        moved = jnp.dot(select, block, preferred_element_type=jnp.float32)
        moved = moved.astype(jnp.bfloat16).reshape(nvt, GROUP, width)
        out_ref[:, 0, pl.ds(part * GROUP, GROUP), :] = moved


def contract(n_tile, per_dev, nvt, ts, width,
             column_ref, sent_ref, w_ref, out_ref,
             tiles, w_raw, w_held, give1, got1, keep, give2, got2,
             tile_send, tile_recv, own_sem, w_sem,
             send1, recv1, send2, recv2):
    me = lax.axis_index("tile")
    slab = lax.axis_index("slab")
    near = slab + 1 - 2 * (slab % 2)
    far = (slab + 2) % 4
    cross = (near + 2) % 4
    rows = out_ref.shape[1]
    count = per_dev
    depth = per_dev * ts
    virtual = nvt * ts

    def tile_copy(q, step):
        there = (me + step) % n_tile
        return pltpu.make_async_remote_copy(
            src_ref=sent_ref.at[there * per_dev + q],
            dst_ref=tiles.at[q, pl.ds(me * depth, depth)],
            send_sem=tile_send.at[q, step],
            recv_sem=tile_recv.at[q, me],
            device_id={"tile": there},
            device_id_type=MESH,
        )

    def tile_arrival(q, step):
        source = (me + step) % n_tile
        return pltpu.make_async_remote_copy(
            src_ref=sent_ref.at[q],
            dst_ref=tiles.at[q, pl.ds(source * depth, depth)],
            send_sem=tile_send.at[q, step],
            recv_sem=tile_recv.at[q, source],
            device_id={"tile": source},
            device_id_type=MESH,
        )

    def own_copy(q):
        return pltpu.make_async_copy(
            sent_ref.at[me * per_dev + q],
            tiles.at[q, pl.ds(me * depth, depth)],
            own_sem.at[q],
        )

    def copy1(slot):
        return pltpu.make_async_remote_copy(
            src_ref=give1.at[slot], dst_ref=got1.at[slot],
            send_sem=send1.at[slot], recv_sem=recv1.at[slot],
            device_id={"slab": near}, device_id_type=MESH,
        )

    def copy2(slot):
        return pltpu.make_async_remote_copy(
            src_ref=give2.at[slot], dst_ref=got2.at[slot],
            send_sem=send2.at[slot], recv_sem=recv2.at[slot],
            device_id={"slab": far}, device_id_type=MESH,
        )

    w_copy = pltpu.make_async_copy(w_ref, w_raw, w_sem)

    barrier = pltpu.get_barrier_semaphore()
    for step in range(1, n_tile):
        pl.semaphore_signal(barrier, inc=1, device_id={"tile": (me + step) % n_tile}, device_id_type=MESH)
    pl.semaphore_signal(barrier, inc=1, device_id={"slab": near}, device_id_type=MESH)
    pl.semaphore_signal(barrier, inc=1, device_id={"slab": far}, device_id_type=MESH)
    pl.semaphore_wait(barrier, n_tile + 1)

    def send_tiles(q):
        for step in range(1, n_tile):
            tile_copy(q, step).start()

    for q in range(min(AHEAD, count)):
        send_tiles(q)
    w_copy.start()
    for q in range(count):
        own_copy(q).start()
    w_copy.wait()

    def reorder(chunk, carry):
        here = pl.ds(pl.multiple_of(chunk * CHUNK, CHUNK), CHUNK)
        line = lax.broadcasted_iota(jnp.int32, (virtual, CHUNK), 0)
        select = jnp.where(line == column_ref[:, here], 1.0, 0.0).astype(jnp.bfloat16)
        for block in range(virtual // rows):
            span = pl.ds(block * rows, rows)
            w_held[span, here] = jnp.dot(
                w_raw[span, :], select, preferred_element_type=jnp.float32
            ).astype(jnp.bfloat16)
        return carry

    lax.fori_loop(0, virtual // CHUNK, reorder, 0)

    def product(q, block):
        return jnp.dot(w_held[pl.ds(pl.multiple_of(block * rows, rows), rows), :], tiles[q],
                       preferred_element_type=jnp.float32)

    def finish(q, slot):
        copy2(slot).wait_recv()
        out_ref[q] = (keep[slot] + got2[slot]).astype(jnp.bfloat16)

    def step(q, carry):
        slot = q % 2
        own_copy(q).wait()
        for other in range(1, n_tile):
            tile_arrival(q, other).wait_recv()

        @pl.when(q + AHEAD < count)
        def _():
            send_tiles(q + AHEAD)

        @pl.when(q >= 2)
        def _():
            copy1(slot).wait_send()

        give1[slot, 0] = product(q, near)
        give1[slot, 1] = product(q, cross)
        copy1(slot).start()

        @pl.when(q >= 1)
        def _():
            finish(q - 1, 1 - slot)

        @pl.when(q >= 2)
        def _():
            copy2(slot).wait_send()

        give2[slot] = product(q, far)
        keep[slot] = product(q, slab)
        copy1(slot).wait_recv()
        give2[slot] = give2[slot] + got1[slot, 1]
        copy2(slot).start()
        keep[slot] = keep[slot] + got1[slot, 0]
        for other in range(1, n_tile):
            tile_copy(q, other).wait_send()
        return carry

    lax.fori_loop(0, count, step, 0)
    finish(count - 1, (count - 1) % 2)
    for q in range(max(count - 2, 0), count):
        copy1(q % 2).wait_send()
        copy2(q % 2).wait_send()


def local(n_tile, n_slab, amps, integrals, tile_mask, amp_map, con_map):
    per_dev, ts, nvt, width = amps.shape[1:]
    virtual = integrals.shape[1]
    rows = virtual // n_slab
    position = lax.axis_index("tile")
    held = lax.dynamic_slice(amp_map, (position * per_dev,), (per_dev,))
    column = (amp_map[:, None] * ts + jnp.arange(ts, dtype=jnp.int32)).reshape(1, virtual)
    alive = jnp.take(jnp.take(tile_mask[0], con_map, axis=0), held, axis=1).T
    shift = nvt * jnp.arange(GROUP, dtype=jnp.int32)
    target = jnp.where(alive[:, :, None] != 0, con_map[None, :, None] + shift, -1)
    target = target.reshape(per_dev, nvt * GROUP, 1).astype(jnp.int32)

    flat = amps.reshape(per_dev * ts * nvt, width)
    ordered = pl.pallas_call(
        functools.partial(arrange, nvt, ts, width),
        grid=(per_dev,),
        out_shape=jax.ShapeDtypeStruct((nvt, per_dev, ts, width), jnp.bfloat16),
        in_specs=[
            pl.BlockSpec((1, nvt * GROUP, 1), lambda p: (p, 0, 0)),
            pl.BlockSpec((ts * nvt, width), lambda p: (p, 0)),
        ],
        out_specs=pl.BlockSpec((nvt, 1, ts, width), lambda p: (0, p, 0, 0)),
        compiler_params=pltpu.CompilerParams(vmem_limit_bytes=40 * 2**20),
    )(target, flat)

    summed = pl.pallas_call(
        functools.partial(contract, n_tile, per_dev, nvt, ts, width),
        out_shape=jax.ShapeDtypeStruct((per_dev, rows, width), jnp.bfloat16),
        in_specs=[
            pl.BlockSpec(memory_space=pltpu.VMEM),
            pl.BlockSpec(memory_space=pl.ANY),
            pl.BlockSpec(memory_space=pl.ANY),
        ],
        out_specs=pl.BlockSpec(memory_space=pltpu.VMEM),
        scratch_shapes=[
            pltpu.VMEM((per_dev, virtual, width), jnp.bfloat16),
            pltpu.VMEM((virtual, virtual), jnp.bfloat16),
            pltpu.VMEM((virtual, virtual), jnp.bfloat16),
            pltpu.VMEM((2, 2, rows, width), jnp.float32),
            pltpu.VMEM((2, 2, rows, width), jnp.float32),
            pltpu.VMEM((2, rows, width), jnp.float32),
            pltpu.VMEM((2, rows, width), jnp.float32),
            pltpu.VMEM((2, rows, width), jnp.float32),
            pltpu.SemaphoreType.DMA((per_dev, n_tile)),
            pltpu.SemaphoreType.DMA((per_dev, n_tile)),
            pltpu.SemaphoreType.DMA((per_dev,)),
            pltpu.SemaphoreType.DMA,
            pltpu.SemaphoreType.DMA((2,)),
            pltpu.SemaphoreType.DMA((2,)),
            pltpu.SemaphoreType.DMA((2,)),
            pltpu.SemaphoreType.DMA((2,)),
        ],
        compiler_params=pltpu.CompilerParams(
            collective_id=0, has_side_effects=True, vmem_limit_bytes=58 * 2**20
        ),
    )(column.astype(jnp.int32), ordered.reshape(nvt, per_dev * ts, width), integrals.reshape(virtual, virtual))
    return jnp.transpose(summed, (1, 0, 2))[:, None]


def solution(mesh):
    in_specs = (
        P("slab", "tile", None, "parts", None),
        P("slab", None, "parts", None),
        P("slab", "parts", None),
        P(),
        P(),
    )
    out_specs = P("slab", "parts", "tile", None)
    body = functools.partial(local, mesh.shape["tile"], mesh.shape["slab"])
    return jax.shard_map(body, mesh=mesh, in_specs=in_specs, out_specs=out_specs, check_vma=False)
```

```python
import functools

import jax
import jax.numpy as jnp
from jax import lax
from jax.experimental import pallas as pl
from jax.experimental.pallas import tpu as pltpu
from jax.sharding import PartitionSpec as P

MESH = pl.DeviceIdType.MESH
GROUP = 16
CHUNK = 256
SPLIT = 2
EARLY = 2
AHEAD = 4


def contract(n_tile, per_dev, nvt, ts, width,
             mask_ref, amp_ref, con_ref, amps_ref, w_ref, out_ref, sent_ref,
             blocks, select, stage, tiles, w_raw, w_held, give1, got1, keep, give2, got2,
             in_sem, stage_sem, tile_send, tile_recv, own_sem, w_sem,
             send1, recv1, send2, recv2):
    me = lax.axis_index("tile")
    slab = lax.axis_index("slab")
    near = slab + 1 - 2 * (slab % 2)
    far = (slab + 2) % 4
    cross = (near + 2) % 4
    rows = out_ref.shape[1]
    piece = width // SPLIT
    count = per_dev * SPLIT
    depth = per_dev * ts
    virtual = nvt * ts
    early = min(EARLY, count)

    def tile_copy(u, step, start=0, size=depth):
        there = (me + step) % n_tile
        return pltpu.make_async_remote_copy(
            src_ref=sent_ref.at[there * per_dev + u // SPLIT, u % SPLIT, pl.ds(start, size)],
            dst_ref=tiles.at[u, pl.ds(me * depth + start, size)],
            send_sem=tile_send.at[u, step],
            recv_sem=tile_recv.at[u, me],
            device_id={"tile": there},
            device_id_type=MESH,
        )

    def tile_arrival(u, step):
        source = (me + step) % n_tile
        return pltpu.make_async_remote_copy(
            src_ref=sent_ref.at[u // SPLIT, u % SPLIT],
            dst_ref=tiles.at[u, pl.ds(source * depth, depth)],
            send_sem=tile_send.at[u, step],
            recv_sem=tile_recv.at[u, source],
            device_id={"tile": source},
            device_id_type=MESH,
        )

    def own_copy(u):
        return pltpu.make_async_copy(
            sent_ref.at[me * per_dev + u // SPLIT, u % SPLIT],
            tiles.at[u, pl.ds(me * depth, depth)],
            own_sem.at[u],
        )

    def copy1(slot):
        return pltpu.make_async_remote_copy(
            src_ref=give1.at[slot], dst_ref=got1.at[slot],
            send_sem=send1.at[slot], recv_sem=recv1.at[slot],
            device_id={"slab": near}, device_id_type=MESH,
        )

    def copy2(slot):
        return pltpu.make_async_remote_copy(
            src_ref=give2.at[slot], dst_ref=got2.at[slot],
            send_sem=send2.at[slot], recv_sem=recv2.at[slot],
            device_id={"slab": far}, device_id_type=MESH,
        )

    def in_copy(p, slot):
        return pltpu.make_async_copy(
            amps_ref.at[pl.ds(p * virtual, virtual)], blocks.at[slot], in_sem.at[slot]
        )

    def stage_copy(p, slot):
        return pltpu.make_async_copy(
            stage.at[slot], sent_ref.at[:, :, pl.ds(p * ts, ts), :], stage_sem.at[slot]
        )

    w_copy = pltpu.make_async_copy(w_ref, w_raw, w_sem)

    barrier = pltpu.get_barrier_semaphore()
    for step in range(1, n_tile):
        pl.semaphore_signal(barrier, inc=1, device_id={"tile": (me + step) % n_tile}, device_id_type=MESH)
    pl.semaphore_signal(barrier, inc=1, device_id={"slab": near}, device_id_type=MESH)
    pl.semaphore_signal(barrier, inc=1, device_id={"slab": far}, device_id_type=MESH)
    in_copy(0, 0).start()
    w_copy.start()
    pl.semaphore_wait(barrier, n_tile + 1)

    def first_sends(p):
        for u in range(early):
            for step in range(1, n_tile):
                tile_copy(u, step, p * ts, ts).start()

    size = GROUP * nvt
    offset = (lax.broadcasted_iota(jnp.int32, (GROUP, size), 1)
              - nvt * lax.broadcasted_iota(jnp.int32, (GROUP, size), 0))

    def arrange(p, carry):
        slot = p % 2

        @pl.when(p + 1 < per_dev)
        def _():
            in_copy(p + 1, 1 - slot).start()

        c_tile = amp_ref[me * per_dev + p]

        def choose(q, inner):
            a_tile = con_ref[q]
            wanted = jnp.where(mask_ref[a_tile, c_tile] != 0, a_tile, -2 * size)
            select[pl.ds(pl.multiple_of(q * GROUP, GROUP), GROUP), :] = jnp.where(
                offset == wanted, 1.0, 0.0).astype(jnp.bfloat16)
            return inner

        lax.fori_loop(0, nvt, choose, 0)
        in_copy(p, slot).wait()
        for part in range(ts // GROUP):
            moved = jnp.dot(select[...], blocks[slot, pl.ds(part * size, size), :],
                            preferred_element_type=jnp.float32)
            moved = moved.astype(jnp.bfloat16).reshape(nvt, GROUP, width)
            for h in range(SPLIT):
                stage[slot, :, h, pl.ds(part * GROUP, GROUP), :] = moved[:, :, h * piece:(h + 1) * piece]
        stage_copy(p, slot).start()

        @pl.when(p >= 1)
        def _():
            stage_copy(p - 1, 1 - slot).wait()
            first_sends(p - 1)

        return carry

    lax.fori_loop(0, per_dev, arrange, 0)
    stage_copy(per_dev - 1, (per_dev - 1) % 2).wait()
    first_sends(per_dev - 1)

    def send_tiles(u):
        for step in range(1, n_tile):
            tile_copy(u, step).start()

    for u in range(early, min(AHEAD, count)):
        send_tiles(u)
    for u in range(count):
        own_copy(u).start()
    w_copy.wait()

    def reorder(chunk, carry):
        here = pl.ds(pl.multiple_of(chunk * CHUNK, CHUNK), CHUNK)
        lane = lax.broadcasted_iota(jnp.int32, (1, CHUNK), 1)
        wanted = lane % ts
        for j in range(CHUNK // ts):
            wanted = wanted + jnp.where(lane // ts == j, amp_ref[chunk * (CHUNK // ts) + j] * ts, 0)
        line = lax.broadcasted_iota(jnp.int32, (virtual, CHUNK), 0)
        pick = jnp.where(line == wanted, 1.0, 0.0).astype(jnp.bfloat16)
        for block in range(virtual // rows):
            span = pl.ds(block * rows, rows)
            w_held[span, here] = jnp.dot(
                w_raw[span, :], pick, preferred_element_type=jnp.float32
            ).astype(jnp.bfloat16)
        return carry

    lax.fori_loop(0, virtual // CHUNK, reorder, 0)

    def product(u, block):
        return jnp.dot(w_held[pl.ds(pl.multiple_of(block * rows, rows), rows), :], tiles[u],
                       preferred_element_type=jnp.float32)

    def finish(u, slot):
        copy2(slot).wait_recv()
        lanes = pl.ds(pl.multiple_of((u % SPLIT) * piece, piece), piece)
        out_ref[u // SPLIT, :, lanes] = (keep[slot] + got2[slot]).astype(jnp.bfloat16)

    def step(u, carry):
        slot = u % 2
        own_copy(u).wait()
        for other in range(1, n_tile):
            tile_arrival(u, other).wait_recv()

        @pl.when(u + AHEAD < count)
        def _():
            send_tiles(u + AHEAD)

        @pl.when(u >= 2)
        def _():
            copy1(slot).wait_send()

        give1[slot, 0] = product(u, near)
        give1[slot, 1] = product(u, cross)
        copy1(slot).start()

        @pl.when(u >= 1)
        def _():
            finish(u - 1, 1 - slot)

        @pl.when(u >= 2)
        def _():
            copy2(slot).wait_send()

        give2[slot] = product(u, far)
        keep[slot] = product(u, slab)
        copy1(slot).wait_recv()
        give2[slot] = give2[slot] + got1[slot, 1]
        copy2(slot).start()
        keep[slot] = keep[slot] + got1[slot, 0]
        for other in range(1, n_tile):
            tile_copy(u, other).wait_send()
        return carry

    lax.fori_loop(0, count, step, 0)
    finish(count - 1, (count - 1) % 2)
    for u in range(max(count - 2, 0), count):
        copy1(u % 2).wait_send()
        copy2(u % 2).wait_send()


def local(n_tile, n_slab, amps, integrals, tile_mask, amp_map, con_map):
    per_dev, ts, nvt, width = amps.shape[1:]
    virtual = integrals.shape[1]
    rows = virtual // n_slab
    piece = width // SPLIT
    count = per_dev * SPLIT
    summed, sent = pl.pallas_call(
        functools.partial(contract, n_tile, per_dev, nvt, ts, width),
        out_shape=(
            jax.ShapeDtypeStruct((per_dev, rows, width), jnp.bfloat16),
            jax.ShapeDtypeStruct((nvt, SPLIT, per_dev * ts, piece), jnp.bfloat16),
        ),
        in_specs=[
            pl.BlockSpec(memory_space=pltpu.SMEM),
            pl.BlockSpec(memory_space=pltpu.SMEM),
            pl.BlockSpec(memory_space=pltpu.SMEM),
            pl.BlockSpec(memory_space=pl.ANY),
            pl.BlockSpec(memory_space=pl.ANY),
        ],
        out_specs=(
            pl.BlockSpec(memory_space=pltpu.VMEM),
            pl.BlockSpec(memory_space=pl.ANY),
        ),
        scratch_shapes=[
            pltpu.VMEM((2, virtual, width), jnp.bfloat16),
            pltpu.VMEM((nvt * GROUP, nvt * GROUP), jnp.bfloat16),
            pltpu.VMEM((2, nvt, SPLIT, ts, piece), jnp.bfloat16),
            pltpu.VMEM((count, virtual, piece), jnp.bfloat16),
            pltpu.VMEM((virtual, virtual), jnp.bfloat16),
            pltpu.VMEM((virtual, virtual), jnp.bfloat16),
            pltpu.VMEM((2, 2, rows, piece), jnp.float32),
            pltpu.VMEM((2, 2, rows, piece), jnp.float32),
            pltpu.VMEM((2, rows, piece), jnp.float32),
            pltpu.VMEM((2, rows, piece), jnp.float32),
            pltpu.VMEM((2, rows, piece), jnp.float32),
            pltpu.SemaphoreType.DMA((2,)),
            pltpu.SemaphoreType.DMA((2,)),
            pltpu.SemaphoreType.DMA((count, n_tile)),
            pltpu.SemaphoreType.DMA((count, n_tile)),
            pltpu.SemaphoreType.DMA((count,)),
            pltpu.SemaphoreType.DMA,
            pltpu.SemaphoreType.DMA((2,)),
            pltpu.SemaphoreType.DMA((2,)),
            pltpu.SemaphoreType.DMA((2,)),
            pltpu.SemaphoreType.DMA((2,)),
        ],
        compiler_params=pltpu.CompilerParams(
            collective_id=0, has_side_effects=True, vmem_limit_bytes=60 * 2**20
        ),
    )(tile_mask[0], amp_map, con_map, amps.reshape(per_dev * virtual, width),
      integrals.reshape(virtual, virtual))
    return jnp.transpose(summed, (1, 0, 2))[:, None]


def solution(mesh):
    in_specs = (
        P("slab", "tile", None, "parts", None),
        P("slab", None, "parts", None),
        P("slab", "parts", None),
        P(),
        P(),
    )
    out_specs = P("slab", "parts", "tile", None)
    body = functools.partial(local, mesh.shape["tile"], mesh.shape["slab"])
    return jax.shard_map(body, mesh=mesh, in_specs=in_specs, out_specs=out_specs, check_vma=False)
```
